256 devices in a mesh: dp: 128 (over z, y, x), tensor: 2 (over core).
Axes of the slice: x: 4, y: 4, z: 8, core: 2. Of those that a mesh axis runs over, the one named last changes fastest.
Arguments:
- x_saved: bfloat16 [2, 32768, 7168], P(None, ('dp', 'tensor')), may hold values from -6 to 6
- grad_pre: bfloat16 [2, 32768, 10240], P(None, 'dp', 'tensor'), may hold values from -6 to 6
- q_prev: float32 [2, 10240, 64], P(None, 'tensor'), may hold values from -6 to 6
Outputs:
- p_hat: float32 [2, 7168, 64], P(None, 'tensor')
- q_new: float32 [2, 10240, 64], P(None, 'tensor')
The draws below stay inside these ranges and needn't reach their ends.
All inputs are finite; a program needn't handle non-finite values.
Results may differ from the reference program's by a relative error of at most 0.018.
Values may be sent and summed in bfloat16 or wider, within the bound.
No kernel may reach another device: no remote copies, remote signals or barrier semaphores. Data moves between devices by JAX's collectives and lax.ppermute only.
A program may use at most 128 MiB of HBM per device.

```python
import jax
import jax.numpy as jnp
from jax import lax

D = 7168
FFW = 10240
RANK = 64
LAYERS = 2
TOKENS = 32768
N_TENSOR = 2


def shard_levels(key, extent, shards, least, high):
    gain, own = 1.0, jax.random.fold_in(key, 6)
    for position, shards_of in shards:
        steps = jnp.exp(jax.random.uniform(jax.random.fold_in(own, position), (shards_of,), jnp.float32, least / len(shards), high / len(shards)))
        gain = gain * jnp.repeat(steps, extent[position] // shards_of).reshape([-1 if axis == position else 1 for axis in range(len(extent))])
    return gain


def centred(own_key, shape, spread, limit, shards=(), dtype=jnp.bfloat16):
    result = jax.random.normal(own_key, shape, jnp.float32) * spread
    if len(shards) > 0:
        result = shard_levels(own_key, shape, shards, -0.22, 0.18) * result
    return jnp.clip(result, min=-limit, max=limit).astype(dtype)


def setup_inputs(seed: int = 0) -> dict:
    keys = jax.random.split(jax.random.key(seed), 4)
    x_saved = centred(keys[0], (LAYERS, TOKENS, D), 1.0, 6.0, ((1, 256),))
    grad_pre = centred(keys[1], (LAYERS, TOKENS, FFW), 1.0, 6.0, ((1, 128), (2, 2)))
    q_prev = centred(keys[2], (LAYERS, FFW, RANK), 1.0, 6.0, ((1, 2),), jnp.float32)
    return {"x_saved": x_saved, "grad_pre": grad_pre, "q_prev": q_prev}


def reference(x_saved, grad_pre, q_prev):
    norm_scale = float(TOKENS) ** (-0.5)
    width = FFW // N_TENSOR
    hat_list = []
    new_list = []
    for layer_index in range(LAYERS):
        half_q = q_prev[layer_index].astype(jnp.bfloat16)
        grad_rows = grad_pre[layer_index]
        summed = jnp.zeros((TOKENS, RANK), jnp.float32)
        for tile_index in range(N_TENSOR):
            piece_sum = jnp.dot(grad_rows[:, tile_index * width:(tile_index + 1) * width].astype(jnp.float32), half_q[tile_index * width:(tile_index + 1) * width].astype(jnp.float32), preferred_element_type=jnp.float32).astype(jnp.bfloat16)
            summed = summed + lax.optimization_barrier(piece_sum).astype(jnp.float32)
        inputs = x_saved[layer_index]
        p_sum = jnp.dot(inputs.astype(jnp.float32).T, summed, precision=lax.Precision.HIGHEST)
        gram_matrix = jnp.dot(p_sum.T, p_sum, precision=lax.Precision.HIGHEST)
        lower_factor = jnp.linalg.cholesky(gram_matrix)
        p_hat = lax.linalg.triangular_solve(lower_factor, p_sum, left_side=False, lower=True, transpose_a=True)
        proj = jnp.dot(inputs.astype(jnp.float32), p_hat.astype(jnp.bfloat16).astype(jnp.float32), preferred_element_type=jnp.float32).astype(jnp.bfloat16)
        q_new = jnp.dot(grad_rows.T.astype(jnp.float32), proj.astype(jnp.float32), preferred_element_type=jnp.float32) * norm_scale
        hat_list.append(p_hat)
        new_list.append(q_new)
    return (jnp.stack(hat_list), jnp.stack(new_list))
```

```python
import jax
import jax.numpy as jnp
from jax import lax
from jax.experimental import pallas as pl
from jax.experimental.pallas import tpu as pltpu
from jax.sharding import Mesh
from jax.sharding import PartitionSpec as P

LANES = 128
NEAR = ("zl", "x", "y")
FAR = ("zh",)
CHIPS = ("zh", "zl", "y", "x")
CORE = "core"
F32, BF16 = jnp.float32, jnp.bfloat16
TRANSPOSED = (((1,), (1,)), ((), ()))


def params(mib):
    return pltpu.CompilerParams(vmem_limit_bytes=mib << 20)


def swap(value):
    return lax.ppermute(value, CORE, [(0, 1), (1, 0)])


def partial_body(grad_ref, q_ref, out_ref, total):
    step = pl.program_id(1)

    @pl.when(step == 0)
    def _():
        total[...] = jnp.zeros_like(total)

    total[...] += lax.dot_general(
        q_ref[0].astype(BF16), grad_ref[0], TRANSPOSED, preferred_element_type=F32
    )

    @pl.when(step == pl.num_programs(1) - 1)
    def _():
        out_ref[0] = total[...].astype(BF16)


def partial_of(grad, q_rows):
    layers, tokens, hidden = grad.shape
    rank = q_rows.shape[1]
    steps = 4
    block = hidden // steps
    return pl.pallas_call(
        partial_body,
        grid=(layers, steps),
        in_specs=[
            pl.BlockSpec((1, tokens, block), lambda l, k: (l, 0, k)),
            pl.BlockSpec((1, rank, block), lambda l, k: (l, 0, k)),
        ],
        out_specs=pl.BlockSpec((1, rank, tokens), lambda l, k: (l, 0, 0)),
        out_shape=jax.ShapeDtypeStruct((layers, rank, tokens), BF16),
        scratch_shapes=[pltpu.VMEM((rank, tokens), F32)],
        compiler_params=params(24),
        name="partial",
    )(grad, q_rows)


def own_first(core, value):
    mid = value.shape[1] // 2
    low, high = value[:, :mid], value[:, mid:]
    return jnp.concatenate(
        [jnp.where(core == 0, low, high), jnp.where(core == 0, high, low)], axis=1
    )


def left_body(core_ref, own_ref, in_ref, mine_ref, theirs_ref, out_ref):
    core = core_ref[0]
    rank = mine_ref.shape[1]
    both = jnp.concatenate(
        [own_first(core, mine_ref[0].astype(F32)), own_first(core, theirs_ref[0].astype(F32))], axis=0
    ).astype(BF16)
    wide = 2 * LANES
    for tile in range(own_ref.shape[2] // wide):
        at = slice(tile * wide, (tile + 1) * wide)
        rows = jnp.concatenate([own_ref[0, :, at], in_ref[0, :, at]], axis=0)
        got = jnp.dot(both, rows, preferred_element_type=F32)
        got = (got[:rank] + got[rank:]).astype(BF16)
        out_ref[0, 2 * tile] = got[:, :LANES]
        out_ref[0, 2 * tile + 1] = got[:, LANES:]


def left_of(core, x_own, x_in, mine, theirs):
    layers, tokens, half = x_in.shape
    rank = mine.shape[1]
    steps = 2
    block = half // steps
    tiles = block // LANES
    return pl.pallas_call(
        left_body,
        grid_spec=pltpu.PrefetchScalarGridSpec(
            num_scalar_prefetch=1,
            grid=(layers, steps),
            in_specs=[
                pl.BlockSpec((1, tokens, block), lambda l, k, c: (l, 0, c[0] * steps + k)),
                pl.BlockSpec((1, tokens, block), lambda l, k, c: (l, 0, k)),
                pl.BlockSpec((1, rank, 2 * tokens), lambda l, k, c: (l, 0, 0)),
                pl.BlockSpec((1, rank, 2 * tokens), lambda l, k, c: (l, 0, 0)),
            ],
            out_specs=pl.BlockSpec((1, tiles, rank, LANES), lambda l, k, c: (l, k, 0, 0)),
        ),
        out_shape=jax.ShapeDtypeStruct((layers, half // LANES, rank, LANES), BF16),
        compiler_params=params(24),
        name="left",
    )(core, x_own, x_in, mine, theirs)


def inner_body(core_ref, own_ref, in_ref, p_ref, out_ref):
    core = core_ref[0]
    layers, tiles, rank = p_ref.shape[:3]
    tokens = 2 * own_ref.shape[1]
    parts, grams = [], []
    for layer in range(layers):
        rows = jnp.concatenate([p_ref[layer, tile] for tile in range(tiles)], axis=1)
        seen = jnp.concatenate([own_ref[layer], in_ref[layer]], axis=0)
        got = lax.dot_general(rows, seen, TRANSPOSED, preferred_element_type=F32)
        parts.append(own_first(core, got))
        grams.append(lax.dot_general(rows, rows, TRANSPOSED, preferred_element_type=F32))
    value = jnp.concatenate(parts + grams, axis=1)

    @pl.when(pl.program_id(0) == 0)
    def _():
        out_ref[...] = value

    @pl.when(pl.program_id(0) > 0)
    def _():
        out_ref[...] += value


def inner_of(core, x_own, x_in, p_blocks):
    layers, tokens, half = x_in.shape
    rank = p_blocks.shape[2]
    steps = 2
    block = half // steps
    tiles = block // LANES
    width = layers * (2 * tokens + rank)
    return pl.pallas_call(
        inner_body,
        grid_spec=pltpu.PrefetchScalarGridSpec(
            num_scalar_prefetch=1,
            grid=(steps,),
            in_specs=[
                pl.BlockSpec((layers, tokens, block), lambda k, c: (0, 0, c[0] * steps + k)),
                pl.BlockSpec((layers, tokens, block), lambda k, c: (0, 0, k)),
                pl.BlockSpec((layers, tiles, rank, LANES), lambda k, c: (0, k, 0, 0)),
            ],
            out_specs=pl.BlockSpec((rank, width), lambda k, c: (0, 0)),
        ),
        out_shape=jax.ShapeDtypeStruct((rank, width), F32),
        compiler_params=params(24),
        name="inner",
    )(core, x_own, x_in, p_blocks)


def inverse_factors(grams, store):
    rank = grams[0].shape[0]
    height = 8
    blocks = rank // height
    line = lax.broadcasted_iota(jnp.int32, (height, rank), 0)
    column = lax.broadcasted_iota(jnp.int32, (height, rank), 1)
    row_id = lax.broadcasted_iota(jnp.int32, (height, 1), 0)
    state = []
    for gram in grams:
        state.append([
            jnp.concatenate(
                [
                    gram[b * height : (b + 1) * height],
                    jnp.where(column == line + b * height, 1.0, 0.0).astype(F32),
                ],
                axis=1,
            )
            for b in range(blocks)
        ])
    for j in range(rank):
        at, low = j // height, j % height
        for index, rows in enumerate(state):
            pivot_row = rows[at][low : low + 1]
            root = lax.rsqrt(pivot_row[:, j : j + 1])
            scaled = pivot_row * root
            store(index, j, scaled[:, rank:])
            for b in range(at, blocks):
                if b == at and low == height - 1:
                    continue
                factor = rows[b][:, j : j + 1] * root
                if b == at:
                    factor = jnp.where(row_id > low, factor, 0.0)
                rows[b] = rows[b] - factor * scaled


def split3(value):
    high = value.astype(BF16)
    rest = value - high.astype(F32)
    mid = rest.astype(BF16)
    return high, mid, (rest - mid.astype(F32)).astype(BF16)


def right_body(scale, mine_ref, theirs_ref, grad_ref, inverse_ref, out_ref, proj):
    layers, rank, tokens = proj.shape

    @pl.when((pl.program_id(0) == 0) & (pl.program_id(1) == 0))
    def _():
        total = mine_ref[...] + theirs_ref[...]
        base = layers * tokens

        def store(layer, row, value):
            inverse_ref[layer, row : row + 1, :] = value

        inverse_factors([total[:, base + l * rank : base + (l + 1) * rank] for l in range(layers)], store)
        for l in range(layers):
            proj[l] = jnp.dot(
                inverse_ref[l],
                total[:, l * tokens : (l + 1) * tokens],
                precision=lax.Precision.HIGHEST,
                preferred_element_type=F32,
            ).astype(BF16)

    left = proj[pl.program_id(0)]
    wide = 2 * LANES
    for tile in range(grad_ref.shape[2] // wide):
        got = jnp.dot(left, grad_ref[0, :, tile * wide : (tile + 1) * wide], preferred_element_type=F32)
        got = (got * scale).astype(BF16)
        out_ref[0, 2 * tile] = got[:, :LANES]
        out_ref[0, 2 * tile + 1] = got[:, LANES:]


def right_of(mine, theirs, grad, scale):
    layers, tokens, hidden = grad.shape
    rank, width = mine.shape
    steps = 4
    block = hidden // steps
    tiles = block // LANES

    def body(*refs):
        right_body(scale, *refs)

    return pl.pallas_call(
        body,
        grid=(layers, steps),
        in_specs=[
            pl.BlockSpec((rank, width), lambda l, k: (0, 0)),
            pl.BlockSpec((rank, width), lambda l, k: (0, 0)),
            pl.BlockSpec((1, tokens, block), lambda l, k: (l, 0, k)),
        ],
        out_specs=[
            pl.BlockSpec((layers, rank, rank), lambda l, k: (0, 0, 0)),
            pl.BlockSpec((1, tiles, rank, LANES), lambda l, k: (l, k, 0, 0)),
        ],
        out_shape=[
            jax.ShapeDtypeStruct((layers, rank, rank), F32),
            jax.ShapeDtypeStruct((layers, hidden // LANES, rank, LANES), BF16),
        ],
        scratch_shapes=[pltpu.VMEM((layers, rank, tokens), BF16)],
        compiler_params=params(24),
        name="right",
    )(mine, theirs, grad)


def hat_body(inverse_ref, p_ref, out_ref):
    rank = inverse_ref.shape[1]
    stacked = jnp.concatenate(split3(inverse_ref[0]), axis=0)
    for tile in range(p_ref.shape[1]):
        got = jnp.dot(stacked, p_ref[0, tile], preferred_element_type=F32)
        got = (got[2 * rank :] + got[rank : 2 * rank]) + got[:rank]
        out_ref[0, :, tile * LANES : (tile + 1) * LANES] = got


def hat_of(inverse, p_blocks):
    layers, tiles, rank, _ = p_blocks.shape
    return pl.pallas_call(
        hat_body,
        grid=(layers,),
        in_specs=[
            pl.BlockSpec((1, rank, rank), lambda l: (l, 0, 0)),
            pl.BlockSpec((1, tiles, rank, LANES), lambda l: (l, 0, 0, 0)),
        ],
        out_specs=pl.BlockSpec((1, rank, tiles * LANES), lambda l: (l, 0, 0)),
        out_shape=jax.ShapeDtypeStruct((layers, rank, tiles * LANES), F32),
        compiler_params=params(24),
        name="hat",
    )(inverse, p_blocks)


def widen_body(in_ref, out_ref):
    for tile in range(in_ref.shape[1]):
        out_ref[0, :, tile * LANES : (tile + 1) * LANES] = in_ref[0, tile].astype(F32)


def widen(blocks):
    layers, tiles, rank, _ = blocks.shape
    steps = 2
    return pl.pallas_call(
        widen_body,
        grid=(layers, steps),
        in_specs=[pl.BlockSpec((1, tiles // steps, rank, LANES), lambda l, k: (l, k, 0, 0))],
        out_specs=pl.BlockSpec((1, rank, tiles // steps * LANES), lambda l, k: (l, 0, k)),
        out_shape=jax.ShapeDtypeStruct((layers, rank, tiles * LANES), F32),
        compiler_params=params(24),
        name="widen",
    )(blocks)


def exchange(value, axes):
    return lax.all_to_all(value, axes, 0, 0, tiled=True)


def add_up(value):
    return jnp.sum(value.astype(F32), axis=0).astype(BF16)


def copies(value, count):
    return jnp.broadcast_to(value[None], (count, *value.shape))


def sum_over_chips(blocks):
    near, far = lax.axis_size(NEAR), lax.axis_size(FAR)
    shape = blocks.shape
    chunks = blocks.reshape(near, -1, LANES)
    chunk = add_up(exchange(chunks, NEAR))
    chunk = add_up(exchange(copies(chunk, far), FAR))
    return exchange(copies(chunk, near), NEAR).reshape(shape)


def on_device(x_saved, grad_pre, q_prev):
    half = x_saved.shape[2] // 2
    token_count = grad_pre.shape[1] * lax.axis_size(CHIPS)
    scale = float(token_count) ** (-0.5)
    core = lax.axis_index(CORE)
    core_array = core.reshape(1)
    x_in = swap(lax.dynamic_slice_in_dim(x_saved, (1 - core) * half, half, axis=2))
    mine = partial_of(grad_pre, jnp.swapaxes(q_prev, 1, 2))
    theirs = swap(mine)
    p_blocks = sum_over_chips(left_of(core_array, x_saved, x_in, mine, theirs))
    inner = inner_of(core_array, x_saved, x_in, p_blocks)
    inverse, q_blocks = right_of(inner, swap(inner), grad_pre, scale)
    p_hat = hat_of(inverse, p_blocks)
    q_new = widen(sum_over_chips(q_blocks))
    return jnp.swapaxes(p_hat, 1, 2), jnp.swapaxes(q_new, 1, 2)


def solution(mesh):
    dims = (4, 2, 4, 4, 2)
    fine = Mesh(mesh.devices.reshape(dims), (*CHIPS, CORE))
    placed = (
        P(None, (*CHIPS, CORE), None),
        P(None, CHIPS, CORE),
        P(None, CORE, None),
    )
    return jax.shard_map(
        on_device,
        mesh=fine,
        in_specs=placed,
        out_specs=(P(None, CORE, None), P(None, CORE, None)),
        check_vma=False,
    )
```

```python
import jax
import jax.numpy as jnp
from jax import lax
from jax.experimental import pallas as pl
from jax.experimental.pallas import tpu as pltpu
from jax.sharding import Mesh
from jax.sharding import PartitionSpec as P

LANES = 128
P_NEAR, Q_NEAR = ("zl", "y", "x"), ("x", "y", "zl")
FAR = ("zh",)
CHIPS = ("zh", "zl", "y", "x")
CORE = "core"
F32, BF16 = jnp.float32, jnp.bfloat16
TRANSPOSED = (((1,), (1,)), ((), ()))
FAR_MEMORY = pl.BlockSpec(memory_space=pltpu.HBM)
WHOLE = pl.BlockSpec(memory_space=pltpu.VMEM)
SCALAR = pl.BlockSpec(memory_space=pltpu.SMEM)


def params(mib):
    return pltpu.CompilerParams(vmem_limit_bytes=mib << 20)


def stay(value):
    return pltpu.with_memory_space_constraint(value, pltpu.HBM)


def near(value):
    return pltpu.with_memory_space_constraint(value, pltpu.VMEM)


def swap(value):
    return lax.ppermute(value, CORE, [(0, 1), (1, 0)])


def half_body(core_ref, x_ref, out_ref, sem):
    half = out_ref.shape[2]
    start = pl.multiple_of((1 - core_ref[0]) * half, LANES)
    move = pltpu.make_async_copy(x_ref.at[:, :, pl.ds(start, half)], out_ref, sem)
    move.start()
    move.wait()


def half_of(core, x):
    layers, tokens, width = x.shape
    return pl.pallas_call(
        half_body,
        in_specs=[SCALAR, FAR_MEMORY],
        out_specs=WHOLE,
        out_shape=pltpu.VMEM((layers, tokens, width // 2), BF16),
        scratch_shapes=[pltpu.SemaphoreType.DMA],
        compiler_params=params(2),
        name="half",
    )(core, stay(x))


def partial_body(core_ref, grad_ref, q_ref, x_ref, out_ref, x_held, grad_held, q_held, sems, x_sem):
    layers, _, hidden = grad_ref.shape
    half = x_held.shape[2]
    steps = sems.shape[2]
    block = hidden // steps
    moves = {}
    for l in range(layers):
        for k in range(steps):
            at = pl.ds(k * block, block)
            for index, (here, held) in enumerate(((q_ref, q_held), (grad_ref, grad_held))):
                moves[l, k, index] = pltpu.make_async_copy(
                    here.at[l, :, at], held.at[l, :, at], sems.at[index, l, k]
                )
                moves[l, k, index].start()
    start = pl.multiple_of(core_ref[0] * half, LANES)
    x_move = pltpu.make_async_copy(x_ref.at[:, :, pl.ds(start, half)], x_held, x_sem)
    x_move.start()
    for l in range(layers):
        total = None
        for k in range(steps):
            moves[l, k, 0].wait()
            moves[l, k, 1].wait()
            at = slice(k * block, (k + 1) * block)
            got = lax.dot_general(
                grad_held[l, :, at], q_held[l, :, at].astype(BF16), TRANSPOSED, preferred_element_type=F32
            )
            total = got if total is None else total + got
        out_ref[l] = total.T.astype(BF16)
    x_move.wait()


def partial_of(core, grad, q_rows, x):
    layers, tokens, hidden = grad.shape
    rank = q_rows.shape[1]
    _, own, width = x.shape
    steps = 4
    return pl.pallas_call(
        partial_body,
        in_specs=[SCALAR, FAR_MEMORY, FAR_MEMORY, FAR_MEMORY],
        out_specs=[WHOLE, WHOLE],
        out_shape=[
            pltpu.VMEM((layers, rank, tokens), BF16),
            pltpu.VMEM((layers, own, width // 2), BF16),
        ],
        scratch_shapes=[
            pltpu.VMEM((layers, tokens, hidden), BF16),
            pltpu.VMEM((layers, rank, hidden), F32),
            pltpu.SemaphoreType.DMA((2, layers, steps)),
            pltpu.SemaphoreType.DMA,
        ],
        compiler_params=params(12),
        name="partial",
    )(core, stay(grad), stay(q_rows), stay(x))


def fetch_body(grad_ref, out_ref, sems):
    moves = [pltpu.make_async_copy(grad_ref.at[l], out_ref.at[l], sems.at[l]) for l in range(out_ref.shape[0])]
    for move in moves:
        move.start()
    for move in moves:
        move.wait()


def fetch(grad):
    return pl.pallas_call(
        fetch_body,
        in_specs=[FAR_MEMORY],
        out_specs=WHOLE,
        out_shape=pltpu.VMEM(grad.shape, BF16),
        scratch_shapes=[pltpu.SemaphoreType.DMA((grad.shape[0],))],
        cost_estimate=pl.CostEstimate(flops=0, bytes_accessed=4 * grad.size, transcendentals=0),
        compiler_params=params(4),
        name="fetch",
    )(stay(grad))


def own_first(core, value):
    mid = value.shape[1] // 2
    low, high = value[:, :mid], value[:, mid:]
    return jnp.concatenate(
        [jnp.where(core == 0, low, high), jnp.where(core == 0, high, low)], axis=1
    )


def left_body(core_ref, own_ref, in_ref, mine_ref, theirs_ref, out_ref):
    core = core_ref[0]
    layers, rank = mine_ref.shape[:2]
    wide = 2 * LANES
    for l in range(layers):
        both = jnp.concatenate(
            [own_first(core, mine_ref[l].astype(F32)), own_first(core, theirs_ref[l].astype(F32))], axis=0
        ).astype(BF16)
        for tile in range(own_ref.shape[2] // wide):
            at = slice(tile * wide, (tile + 1) * wide)
            rows = jnp.concatenate([own_ref[l, :, at], in_ref[l, :, at]], axis=0)
            got = jnp.dot(both, rows, preferred_element_type=F32)
            got = (got[:rank] + got[rank:]).astype(BF16)
            out_ref[l, 2 * tile] = got[:, :LANES]
            out_ref[l, 2 * tile + 1] = got[:, LANES:]


def left_of(core, x_own, x_in, mine, theirs):
    layers, _, half = x_in.shape
    rank = mine.shape[1]
    return pl.pallas_call(
        left_body,
        in_specs=[SCALAR, WHOLE, WHOLE, WHOLE, WHOLE],
        out_specs=WHOLE,
        out_shape=pltpu.VMEM((layers, half // LANES, rank, LANES), BF16),
        compiler_params=params(6),
        name="left",
    )(core, near(x_own), near(x_in), near(mine), near(theirs))


def inner_body(core_ref, own_ref, in_ref, p_ref, out_ref):
    core = core_ref[0]
    layers, tiles, rank, _ = p_ref.shape
    tokens = 2 * own_ref.shape[1]
    base = layers * tokens
    for l in range(layers):
        rows = jnp.concatenate([p_ref[l, tile] for tile in range(tiles)], axis=1)
        seen = jnp.concatenate([own_ref[l], in_ref[l]], axis=0)
        got = lax.dot_general(rows, seen, TRANSPOSED, preferred_element_type=F32)
        out_ref[:, l * tokens : (l + 1) * tokens] = own_first(core, got)
        got = lax.dot_general(rows, rows, TRANSPOSED, preferred_element_type=F32)
        out_ref[:, base + l * rank : base + (l + 1) * rank] = got


def inner_of(core, x_own, x_in, p_blocks):
    layers, tokens, _ = x_in.shape
    rank = p_blocks.shape[2]
    width = layers * (2 * tokens + rank)
    return pl.pallas_call(
        inner_body,
        in_specs=[SCALAR, WHOLE, WHOLE, WHOLE],
        out_specs=WHOLE,
        out_shape=pltpu.VMEM((rank, width), F32),
        compiler_params=params(8),
        name="inner",
    )(core, near(x_own), near(x_in), near(p_blocks))


def inverse_factors(grams, store):
    rank = grams[0].shape[0]
    height = 8
    blocks = rank // height
    shape = (height, 2 * rank)
    line = lax.broadcasted_iota(jnp.int32, (height, rank), 0)
    column = lax.broadcasted_iota(jnp.int32, (height, rank), 1)
    state = [
        [
            jnp.concatenate(
                [
                    gram[b * height : (b + 1) * height],
                    jnp.where(column == line + b * height, 1.0, 0.0).astype(F32),
                ],
                axis=1,
            )
            for b in range(blocks)
        ]
        for gram in grams
    ]

    def full(value):
        return jnp.broadcast_to(value, shape)

    for at in range(blocks):
        first = at * height
        for index, rows in enumerate(state):
            pivots = [full(rows[at][k : k + 1]) for k in range(height)]
            corners = {
                (k, m): full(pivots[k][:, first + m : first + m + 1]) for k in range(height) for m in range(k, height)
            }
            columns = {
                b: [full(rows[b][:, first + k : first + k + 1]) for k in range(height)]
                for b in range(at + 1, blocks)
            }
            scaled, roots, factors = [], [], {}
            for k in range(height):
                corner, row = corners[k, k], pivots[k]
                for q in range(k):
                    corner = corner - factors[q, k] * factors[q, k]
                roots.append(lax.rsqrt(corner))
                for q in range(k):
                    row = row - factors[q, k] * scaled[q]
                scaled.append(row * roots[k])
                for m in range(k + 1, height):
                    value = corners[k, m]
                    for q in range(k):
                        value = value - factors[q, k] * factors[q, m]
                    factors[k, m] = value * roots[k]
            for k in range(height):
                store(index, first + k, scaled[k][:1, rank:])
            for b in range(at + 1, blocks):
                lower = []
                for k in range(height):
                    value = columns[b][k]
                    for q in range(k):
                        value = value - lower[q] * factors[q, k]
                    lower.append(value * roots[k])
                for k in range(height):
                    rows[b] = rows[b] - lower[k] * scaled[k]


def split3(value):
    high = value.astype(BF16)
    rest = value - high.astype(F32)
    mid = rest.astype(BF16)
    return high, mid, (rest - mid.astype(F32)).astype(BF16)


def right_body(scale, mine_ref, theirs_ref, grad_ref, inverse_ref, out_ref):
    layers, tokens, hidden = grad_ref.shape
    rank = mine_ref.shape[0]
    total = mine_ref[...] + theirs_ref[...]
    base = layers * tokens

    def store(layer, row, value):
        inverse_ref[layer, row : row + 1, :] = value

    inverse_factors([total[:, base + l * rank : base + (l + 1) * rank] for l in range(layers)], store)
    wide = 2 * LANES
    for l in range(layers):
        left = jnp.dot(
            inverse_ref[l],
            total[:, l * tokens : (l + 1) * tokens],
            precision=lax.Precision.HIGHEST,
            preferred_element_type=F32,
        ).astype(BF16)
        for tile in range(hidden // wide):
            got = jnp.dot(left, grad_ref[l, :, tile * wide : (tile + 1) * wide], preferred_element_type=F32)
            got = (got * scale).astype(BF16)
            out_ref[l, 2 * tile] = got[:, :LANES]
            out_ref[l, 2 * tile + 1] = got[:, LANES:]


def right_of(mine, theirs, grad, scale):
    layers, _, hidden = grad.shape
    rank, _ = mine.shape

    def body(*refs):
        right_body(scale, *refs)

    return pl.pallas_call(
        body,
        in_specs=[WHOLE, WHOLE, WHOLE],
        out_specs=[WHOLE, WHOLE],
        out_shape=[
            pltpu.VMEM((layers, rank, rank), F32),
            pltpu.VMEM((layers, hidden // LANES, rank, LANES), BF16),
        ],
        compiler_params=params(8),
        name="right",
    )(near(mine), near(theirs), near(grad))


def finish_body(inverse_ref, p_ref, q_ref, hat_ref, new_ref):
    rank = inverse_ref.shape[1]
    wide = 2 * LANES
    for tile in range(q_ref.shape[1]):
        new_ref[0, :, tile * LANES : (tile + 1) * LANES] = q_ref[0, tile].astype(F32)
    stacked = jnp.concatenate(split3(inverse_ref[0]), axis=0)
    for tile in range(p_ref.shape[1] // 2):
        rows = jnp.concatenate([p_ref[0, 2 * tile], p_ref[0, 2 * tile + 1]], axis=1)
        got = jnp.dot(stacked, rows, preferred_element_type=F32)
        got = (got[2 * rank :] + got[rank : 2 * rank]) + got[:rank]
        hat_ref[0, :, tile * wide : (tile + 1) * wide] = got


def finish(inverse, p_blocks, q_blocks):
    layers, p_tiles, rank, _ = p_blocks.shape
    q_tiles = q_blocks.shape[1]
    steps = 2
    return pl.pallas_call(
        finish_body,
        grid=(layers, steps),
        in_specs=[
            pl.BlockSpec((1, rank, rank), lambda l, k: (l, 0, 0)),
            pl.BlockSpec((1, p_tiles // steps, rank, LANES), lambda l, k: (l, k, 0, 0)),
            pl.BlockSpec((1, q_tiles // steps, rank, LANES), lambda l, k: (l, k, 0, 0)),
        ],
        out_specs=[
            pl.BlockSpec((1, rank, p_tiles // steps * LANES), lambda l, k: (l, 0, k)),
            pl.BlockSpec((1, rank, q_tiles // steps * LANES), lambda l, k: (l, 0, k)),
        ],
        out_shape=[
            jax.ShapeDtypeStruct((layers, rank, p_tiles * LANES), F32),
            jax.ShapeDtypeStruct((layers, rank, q_tiles * LANES), F32),
        ],
        compiler_params=params(12),
        name="finish",
    )(inverse, p_blocks, q_blocks)


def exchange(value, axes):
    return lax.all_to_all(value, axes, 0, 0, tiled=True)


def add_up(value):
    return jnp.sum(value.astype(F32), axis=0).astype(BF16)


def copies(value, count):
    return jnp.broadcast_to(value[None], (count, *value.shape))


def sum_over_chips(blocks, group):
    inside, outside = lax.axis_size(group), lax.axis_size(FAR)
    shape = blocks.shape
    chunks = blocks.reshape(inside, -1, LANES)
    chunk = add_up(exchange(chunks, group))
    chunk = add_up(exchange(copies(chunk, outside), FAR))
    return exchange(copies(chunk, inside), group).reshape(shape)


def on_device(x_saved, grad_pre, q_prev):
    token_count = grad_pre.shape[1] * lax.axis_size(CHIPS)
    scale = float(token_count) ** (-0.5)
    core = lax.axis_index(CORE)
    core_array = core.reshape(1)
    x_in = swap(half_of(core_array, x_saved))
    mine, x_own = partial_of(core_array, grad_pre, jnp.swapaxes(q_prev, 1, 2), x_saved)
    theirs = swap(mine)
    p_blocks = sum_over_chips(left_of(core_array, x_own, x_in, mine, theirs), P_NEAR)
    inner = inner_of(core_array, x_own, x_in, p_blocks)
    grad, tied = lax.optimization_barrier((grad_pre, inner))
    inverse, q_blocks = right_of(tied, swap(tied), fetch(grad), scale)
    p_hat, q_new = finish(inverse, p_blocks, sum_over_chips(q_blocks, Q_NEAR))
    return jnp.swapaxes(p_hat, 1, 2), jnp.swapaxes(q_new, 1, 2)


def solution(mesh):
    dims = (4, 2, 4, 4, 2)
    fine = Mesh(mesh.devices.reshape(dims), (*CHIPS, CORE))
    placed = (
        P(None, (*CHIPS, CORE), None),
        P(None, CHIPS, CORE),
        P(None, CORE, None),
    )
    return jax.shard_map(
        on_device,
        mesh=fine,
        in_specs=placed,
        out_specs=(P(None, CORE, None), P(None, CORE, None)),
        check_vma=False,
    )
```

```python
import jax
import jax.numpy as jnp
from jax import lax
from jax.experimental import pallas as pl
from jax.experimental.pallas import tpu as pltpu
from jax.sharding import Mesh
from jax.sharding import PartitionSpec as P

LANES = 128
P_NEAR, Q_NEAR = ("zl", "y", "x"), ("x", "y", "zl")
FAR = ("zh",)
CHIPS = ("zh", "zl", "y", "x")
CORE = "core"
F32, BF16 = jnp.float32, jnp.bfloat16
TRANSPOSED = (((1,), (1,)), ((), ()))
FAR_MEMORY = pl.BlockSpec(memory_space=pltpu.HBM)
WHOLE = pl.BlockSpec(memory_space=pltpu.VMEM)
SCALAR = pl.BlockSpec(memory_space=pltpu.SMEM)


def params(mib):
    return pltpu.CompilerParams(vmem_limit_bytes=mib << 20)


def stay(value):
    return pltpu.with_memory_space_constraint(value, pltpu.HBM)


def near(value):
    return pltpu.with_memory_space_constraint(value, pltpu.VMEM)


def swap(value):
    return lax.ppermute(value, CORE, [(0, 1), (1, 0)])


def half_body(core_ref, x_ref, out_ref, sem):
    half = out_ref.shape[2]
    start = pl.multiple_of((1 - core_ref[0]) * half, LANES)
    move = pltpu.make_async_copy(x_ref.at[:, :, pl.ds(start, half)], out_ref, sem)
    move.start()
    move.wait()


def half_of(core, x):
    layers, tokens, width = x.shape
    return pl.pallas_call(
        half_body,
        in_specs=[SCALAR, FAR_MEMORY],
        out_specs=WHOLE,
        out_shape=pltpu.VMEM((layers, tokens, width // 2), BF16),
        scratch_shapes=[pltpu.SemaphoreType.DMA],
        compiler_params=params(2),
        name="half",
    )(core, stay(x))


def partial_body(core_ref, grad_ref, q_ref, x_ref, out_ref, x_held, grad_held, q_held, sems, x_sem):
    layers, _, hidden = grad_ref.shape
    half = x_held.shape[2]
    steps = sems.shape[2]
    block = hidden // steps
    moves = {}
    for l in range(layers):
        for k in range(steps):
            at = pl.ds(k * block, block)
            for index, (here, held) in enumerate(((q_ref, q_held), (grad_ref, grad_held))):
                moves[l, k, index] = pltpu.make_async_copy(
                    here.at[l, :, at], held.at[l, :, at], sems.at[index, l, k]
                )
                moves[l, k, index].start()
    start = pl.multiple_of(core_ref[0] * half, LANES)
    x_move = pltpu.make_async_copy(x_ref.at[:, :, pl.ds(start, half)], x_held, x_sem)
    x_move.start()
    for l in range(layers):
        total = None
        for k in range(steps):
            moves[l, k, 0].wait()
            moves[l, k, 1].wait()
            at = slice(k * block, (k + 1) * block)
            got = lax.dot_general(
                grad_held[l, :, at], q_held[l, :, at].astype(BF16), TRANSPOSED, preferred_element_type=F32
            )
            total = got if total is None else total + got
        out_ref[l] = total.T.astype(BF16)
    x_move.wait()


def partial_of(core, grad, q_rows, x):
    layers, tokens, hidden = grad.shape
    rank = q_rows.shape[1]
    _, own, width = x.shape
    steps = 4
    return pl.pallas_call(
        partial_body,
        in_specs=[SCALAR, FAR_MEMORY, FAR_MEMORY, FAR_MEMORY],
        out_specs=[WHOLE, WHOLE],
        out_shape=[
            pltpu.VMEM((layers, rank, tokens), BF16),
            pltpu.VMEM((layers, own, width // 2), BF16),
        ],
        scratch_shapes=[
            pltpu.VMEM((layers, tokens, hidden), BF16),
            pltpu.VMEM((layers, rank, hidden), F32),
            pltpu.SemaphoreType.DMA((2, layers, steps)),
            pltpu.SemaphoreType.DMA,
        ],
        compiler_params=params(12),
        name="partial",
    )(core, stay(grad), stay(q_rows), stay(x))


def fetch_body(grad_ref, out_ref, sems):
    moves = [pltpu.make_async_copy(grad_ref.at[l], out_ref.at[l], sems.at[l]) for l in range(out_ref.shape[0])]
    for move in moves:
        move.start()
    for move in moves:
        move.wait()


def fetch(grad):
    return pl.pallas_call(
        fetch_body,
        in_specs=[FAR_MEMORY],
        out_specs=WHOLE,
        out_shape=pltpu.VMEM(grad.shape, BF16),
        scratch_shapes=[pltpu.SemaphoreType.DMA((grad.shape[0],))],
        cost_estimate=pl.CostEstimate(flops=0, bytes_accessed=4 * grad.size, transcendentals=0),
        compiler_params=params(4),
        name="fetch",
    )(stay(grad))


def own_first(core, value):
    mid = value.shape[1] // 2
    low, high = value[:, :mid], value[:, mid:]
    return jnp.concatenate(
        [jnp.where(core == 0, low, high), jnp.where(core == 0, high, low)], axis=1
    )


def left_body(core_ref, own_ref, in_ref, mine_ref, theirs_ref, out_ref):
    core = core_ref[0]
    layers, rank = mine_ref.shape[:2]
    wide = 2 * LANES
    for l in range(layers):
        both = jnp.concatenate(
            [own_first(core, mine_ref[l].astype(F32)), own_first(core, theirs_ref[l].astype(F32))], axis=0
        ).astype(BF16)
        for tile in range(own_ref.shape[2] // wide):
            at = slice(tile * wide, (tile + 1) * wide)
            rows = jnp.concatenate([own_ref[l, :, at], in_ref[l, :, at]], axis=0)
            got = jnp.dot(both, rows, preferred_element_type=F32)
            got = (got[:rank] + got[rank:]).astype(BF16)
            out_ref[l, 2 * tile] = got[:, :LANES]
            out_ref[l, 2 * tile + 1] = got[:, LANES:]


def left_of(core, x_own, x_in, mine, theirs):
    layers, _, half = x_in.shape
    rank = mine.shape[1]
    return pl.pallas_call(
        left_body,
        in_specs=[SCALAR, WHOLE, WHOLE, WHOLE, WHOLE],
        out_specs=WHOLE,
        out_shape=pltpu.VMEM((layers, half // LANES, rank, LANES), BF16),
        compiler_params=params(6),
        name="left",
    )(core, near(x_own), near(x_in), near(mine), near(theirs))


def rows_of(p_ref, layer):
    return jnp.concatenate([p_ref[layer, tile] for tile in range(p_ref.shape[1])], axis=1)


def gram_body(p_ref, out_ref):
    rank = p_ref.shape[2]
    for l in range(p_ref.shape[0]):
        rows = rows_of(p_ref, l)
        got = lax.dot_general(rows, rows, TRANSPOSED, preferred_element_type=F32)
        out_ref[:, l * rank : (l + 1) * rank] = got


def gram_of(p_blocks):
    layers, _, rank, _ = p_blocks.shape
    return pl.pallas_call(
        gram_body,
        in_specs=[WHOLE],
        out_specs=WHOLE,
        out_shape=pltpu.VMEM((rank, layers * rank), F32),
        cost_estimate=pl.CostEstimate(flops=2 * rank * p_blocks.size, bytes_accessed=2 * p_blocks.size, transcendentals=0),
        compiler_params=params(8),
        name="gram",
    )(near(p_blocks))


def inner_body(core_ref, own_ref, in_ref, p_ref, out_ref):
    core = core_ref[0]
    tokens = 2 * own_ref.shape[1]
    for l in range(p_ref.shape[0]):
        seen = jnp.concatenate([own_ref[l], in_ref[l]], axis=0)
        got = lax.dot_general(rows_of(p_ref, l), seen, TRANSPOSED, preferred_element_type=F32)
        out_ref[:, l * tokens : (l + 1) * tokens] = own_first(core, got)


def inner_of(core, x_own, x_in, p_blocks):
    layers, tokens, half = x_in.shape
    rank = p_blocks.shape[2]
    return pl.pallas_call(
        inner_body,
        in_specs=[SCALAR, WHOLE, WHOLE, WHOLE],
        out_specs=WHOLE,
        out_shape=pltpu.VMEM((rank, 2 * layers * tokens), F32),
        cost_estimate=pl.CostEstimate(flops=4 * rank * x_in.size, bytes_accessed=6 * x_in.size, transcendentals=0),
        compiler_params=params(8),
        name="inner",
    )(core, near(x_own), near(x_in), near(p_blocks))


def inverse_factors(grams, store):
    rank = grams[0].shape[0]
    height = 8
    blocks = rank // height
    shape = (height, 2 * rank)
    line = lax.broadcasted_iota(jnp.int32, (height, rank), 0)
    column = lax.broadcasted_iota(jnp.int32, (height, rank), 1)
    state = [
        [
            jnp.concatenate(
                [
                    gram[b * height : (b + 1) * height],
                    jnp.where(column == line + b * height, 1.0, 0.0).astype(F32),
                ],
                axis=1,
            )
            for b in range(blocks)
        ]
        for gram in grams
    ]

    def full(value):
        return jnp.broadcast_to(value, shape)

    for at in range(blocks):
        first = at * height
        for index, rows in enumerate(state):
            pivots = [full(rows[at][k : k + 1]) for k in range(height)]
            corners = {
                (k, m): full(pivots[k][:, first + m : first + m + 1]) for k in range(height) for m in range(k, height)
            }
            columns = {
                b: [full(rows[b][:, first + k : first + k + 1]) for k in range(height)]
                for b in range(at + 1, blocks)
            }
            scaled, roots, factors = [], [], {}
            for k in range(height):
                corner, row = corners[k, k], pivots[k]
                for q in range(k):
                    corner = corner - factors[q, k] * factors[q, k]
                roots.append(lax.rsqrt(corner))
                for q in range(k):
                    row = row - factors[q, k] * scaled[q]
                scaled.append(row * roots[k])
                for m in range(k + 1, height):
                    value = corners[k, m]
                    for q in range(k):
                        value = value - factors[q, k] * factors[q, m]
                    factors[k, m] = value * roots[k]
            for k in range(height):
                store(index, first + k, scaled[k][:1, rank:])
            for b in range(at + 1, blocks):
                lower = []
                for k in range(height):
                    value = columns[b][k]
                    for q in range(k):
                        value = value - lower[q] * factors[q, k]
                    lower.append(value * roots[k])
                for k in range(height):
                    rows[b] = rows[b] - lower[k] * scaled[k]


def split3(value):
    high = value.astype(BF16)
    rest = value - high.astype(F32)
    mid = rest.astype(BF16)
    return high, mid, (rest - mid.astype(F32)).astype(BF16)


def factor_body(mine_ref, theirs_ref, inverse_ref):
    layers, rank, _ = inverse_ref.shape
    total = mine_ref[...] + theirs_ref[...]

    def store(layer, row, value):
        inverse_ref[layer, row : row + 1, :] = value

    inverse_factors([total[:, l * rank : (l + 1) * rank] for l in range(layers)], store)


def factor_of(mine, theirs):
    rank, width = mine.shape
    return pl.pallas_call(
        factor_body,
        in_specs=[WHOLE, WHOLE],
        out_specs=WHOLE,
        out_shape=pltpu.VMEM((width // rank, rank, rank), F32),
        cost_estimate=pl.CostEstimate(flops=10**9, bytes_accessed=10**6, transcendentals=0),
        compiler_params=params(8),
        name="factor",
    )(near(mine), near(theirs))


def right_body(scale, inverse_ref, mine_ref, theirs_ref, grad_ref, out_ref):
    layers, tokens, hidden = grad_ref.shape
    wide = 2 * LANES
    for l in range(layers):
        at = slice(l * tokens, (l + 1) * tokens)
        left = jnp.dot(
            inverse_ref[l],
            mine_ref[:, at] + theirs_ref[:, at],
            precision=lax.Precision.HIGHEST,
            preferred_element_type=F32,
        ).astype(BF16)
        for tile in range(hidden // wide):
            got = jnp.dot(left, grad_ref[l, :, tile * wide : (tile + 1) * wide], preferred_element_type=F32)
            got = (got * scale).astype(BF16)
            out_ref[l, 2 * tile] = got[:, :LANES]
            out_ref[l, 2 * tile + 1] = got[:, LANES:]


def right_of(inverse, mine, theirs, grad, scale):
    layers, _, hidden = grad.shape
    rank, _ = mine.shape

    def body(*refs):
        right_body(scale, *refs)

    return pl.pallas_call(
        body,
        in_specs=[WHOLE, WHOLE, WHOLE, WHOLE],
        out_specs=WHOLE,
        out_shape=pltpu.VMEM((layers, hidden // LANES, rank, LANES), BF16),
        compiler_params=params(8),
        name="right",
    )(near(inverse), near(mine), near(theirs), near(grad))


def finish_body(inverse_ref, p_ref, q_ref, hat_ref, new_ref):
    rank = inverse_ref.shape[1]
    wide = 2 * LANES
    for tile in range(q_ref.shape[1]):
        new_ref[0, :, tile * LANES : (tile + 1) * LANES] = q_ref[0, tile].astype(F32)
    stacked = jnp.concatenate(split3(inverse_ref[0]), axis=0)
    for tile in range(p_ref.shape[1] // 2):
        rows = jnp.concatenate([p_ref[0, 2 * tile], p_ref[0, 2 * tile + 1]], axis=1)
        got = jnp.dot(stacked, rows, preferred_element_type=F32)
        got = (got[2 * rank :] + got[rank : 2 * rank]) + got[:rank]
        hat_ref[0, :, tile * wide : (tile + 1) * wide] = got


def finish(inverse, p_blocks, q_blocks):
    layers, p_tiles, rank, _ = p_blocks.shape
    q_tiles = q_blocks.shape[1]
    steps = 2
    return pl.pallas_call(
        finish_body,
        grid=(layers, steps),
        in_specs=[
            pl.BlockSpec((1, rank, rank), lambda l, k: (l, 0, 0)),
            pl.BlockSpec((1, p_tiles // steps, rank, LANES), lambda l, k: (l, k, 0, 0)),
            pl.BlockSpec((1, q_tiles // steps, rank, LANES), lambda l, k: (l, k, 0, 0)),
        ],
        out_specs=[
            pl.BlockSpec((1, rank, p_tiles // steps * LANES), lambda l, k: (l, 0, k)),
            pl.BlockSpec((1, rank, q_tiles // steps * LANES), lambda l, k: (l, 0, k)),
        ],
        out_shape=[
            jax.ShapeDtypeStruct((layers, rank, p_tiles * LANES), F32),
            jax.ShapeDtypeStruct((layers, rank, q_tiles * LANES), F32),
        ],
        compiler_params=params(12),
        name="finish",
    )(inverse, p_blocks, q_blocks)


def exchange(value, axes):
    return lax.all_to_all(value, axes, 0, 0, tiled=True)


def add_up(value):
    return jnp.sum(value.astype(F32), axis=0).astype(BF16)


def copies(value, count):
    return jnp.broadcast_to(value[None], (count, *value.shape))


def sum_over_chips(blocks, group):
    inside, outside = lax.axis_size(group), lax.axis_size(FAR)
    shape = blocks.shape
    chunks = blocks.reshape(inside, -1, LANES)
    chunk = add_up(exchange(chunks, group))
    chunk = add_up(exchange(copies(chunk, outside), FAR))
    return exchange(copies(chunk, inside), group).reshape(shape)


def on_device(x_saved, grad_pre, q_prev):
    token_count = grad_pre.shape[1] * lax.axis_size(CHIPS)
    scale = float(token_count) ** (-0.5)
    core = lax.axis_index(CORE)
    core_array = core.reshape(1)
    x_in = swap(half_of(core_array, x_saved))
    mine, x_own = partial_of(core_array, grad_pre, jnp.swapaxes(q_prev, 1, 2), x_saved)
    theirs = swap(mine)
    p_blocks = sum_over_chips(left_of(core_array, x_own, x_in, mine, theirs), P_NEAR)
    gram = gram_of(p_blocks)
    grad, gram = lax.optimization_barrier((grad_pre, gram))
    inner = inner_of(core_array, x_own, x_in, p_blocks)
    held = fetch(grad)
    inverse = factor_of(gram, swap(gram))
    q_blocks = right_of(inverse, inner, swap(inner), held, scale)
    p_hat, q_new = finish(inverse, p_blocks, sum_over_chips(q_blocks, Q_NEAR))
    return jnp.swapaxes(p_hat, 1, 2), jnp.swapaxes(q_new, 1, 2)


def solution(mesh):
    dims = (4, 2, 4, 4, 2)
    fine = Mesh(mesh.devices.reshape(dims), (*CHIPS, CORE))
    placed = (
        P(None, (*CHIPS, CORE), None),
        P(None, CHIPS, CORE),
        P(None, CORE, None),
    )
    return jax.shard_map(
        on_device,
        mesh=fine,
        in_specs=placed,
        out_specs=(P(None, CORE, None), P(None, CORE, None)),
        check_vma=False,
    )
```

```python
import jax
import jax.numpy as jnp
from jax import lax
from jax.experimental import pallas as pl
from jax.experimental.pallas import tpu as pltpu
from jax.sharding import Mesh
from jax.sharding import PartitionSpec as P

LANES = 128
P_NEAR, Q_NEAR = ("zl", "y", "x"), ("x", "y", "zl")
FAR = ("zh",)
CHIPS = ("zh", "zl", "y", "x")
CORE = "core"
F32, BF16 = jnp.float32, jnp.bfloat16
TRANSPOSED = (((1,), (1,)), ((), ()))
FAR_MEMORY = pl.BlockSpec(memory_space=pltpu.HBM)
WHOLE = pl.BlockSpec(memory_space=pltpu.VMEM)
SCALAR = pl.BlockSpec(memory_space=pltpu.SMEM)


def params(mib):
    return pltpu.CompilerParams(vmem_limit_bytes=mib << 20)


def stay(value):
    return pltpu.with_memory_space_constraint(value, pltpu.HBM)


def near(value):
    return pltpu.with_memory_space_constraint(value, pltpu.VMEM)


def swap(value):
    return lax.ppermute(value, CORE, [(0, 1), (1, 0)])


def half_body(core_ref, x_ref, out_ref, sem):
    half = out_ref.shape[2]
    start = pl.multiple_of((1 - core_ref[0]) * half, LANES)
    move = pltpu.make_async_copy(x_ref.at[:, :, pl.ds(start, half)], out_ref, sem)
    move.start()
    move.wait()


def half_of(core, x):
    layers, tokens, width = x.shape
    return pl.pallas_call(
        half_body,
        in_specs=[SCALAR, FAR_MEMORY],
        out_specs=WHOLE,
        out_shape=pltpu.VMEM((layers, tokens, width // 2), BF16),
        scratch_shapes=[pltpu.SemaphoreType.DMA],
        compiler_params=params(2),
        name="half",
    )(core, stay(x))


def partial_body(core_ref, grad_ref, q_ref, x_ref, out_ref, x_held, grad_held, q_held, sems, x_sem):
    layers, _, hidden = grad_ref.shape
    half = x_held.shape[2]
    steps = sems.shape[2]
    block = hidden // steps
    moves = {}
    for l in range(layers):
        for k in range(steps):
            at = pl.ds(k * block, block)
            for index, (here, held) in enumerate(((q_ref, q_held), (grad_ref, grad_held))):
                moves[l, k, index] = pltpu.make_async_copy(
                    here.at[l, :, at], held.at[l, :, at], sems.at[index, l, k]
                )
                moves[l, k, index].start()
    start = pl.multiple_of(core_ref[0] * half, LANES)
    x_move = pltpu.make_async_copy(x_ref.at[:, :, pl.ds(start, half)], x_held, x_sem)
    x_move.start()
    for l in range(layers):
        total = None
        for k in range(steps):
            moves[l, k, 0].wait()
            moves[l, k, 1].wait()
            at = slice(k * block, (k + 1) * block)
            got = lax.dot_general(
                grad_held[l, :, at], q_held[l, :, at].astype(BF16), TRANSPOSED, preferred_element_type=F32
            )
            total = got if total is None else total + got
        out_ref[l] = total.T.astype(BF16)
    x_move.wait()


def partial_of(core, grad, q_rows, x):
    layers, tokens, hidden = grad.shape
    rank = q_rows.shape[1]
    _, own, width = x.shape
    steps = 4
    return pl.pallas_call(
        partial_body,
        in_specs=[SCALAR, FAR_MEMORY, FAR_MEMORY, FAR_MEMORY],
        out_specs=[WHOLE, WHOLE],
        out_shape=[
            pltpu.VMEM((layers, rank, tokens), BF16),
            pltpu.VMEM((layers, own, width // 2), BF16),
        ],
        scratch_shapes=[
            pltpu.VMEM((layers, tokens, hidden), BF16),
            pltpu.VMEM((layers, rank, hidden), F32),
            pltpu.SemaphoreType.DMA((2, layers, steps)),
            pltpu.SemaphoreType.DMA,
        ],
        compiler_params=params(12),
        name="partial",
    )(core, stay(grad), stay(q_rows), stay(x))


def fetch_body(grad_ref, out_ref, sem):
    move = pltpu.make_async_copy(grad_ref.at[0], out_ref, sem)
    move.start()
    move.wait()


def fetch(grad):
    return pl.pallas_call(
        fetch_body,
        in_specs=[FAR_MEMORY],
        out_specs=WHOLE,
        out_shape=pltpu.VMEM(grad.shape[1:], BF16),
        scratch_shapes=[pltpu.SemaphoreType.DMA],
        cost_estimate=pl.CostEstimate(flops=0, bytes_accessed=2 * grad.size, transcendentals=0),
        compiler_params=params(4),
        name="fetch",
    )(stay(grad))


def own_first(core, value):
    mid = value.shape[1] // 2
    low, high = value[:, :mid], value[:, mid:]
    return jnp.concatenate(
        [jnp.where(core == 0, low, high), jnp.where(core == 0, high, low)], axis=1
    )


def left_body(core_ref, own_ref, in_ref, mine_ref, theirs_ref, out_ref):
    core = core_ref[0]
    layers, rank = mine_ref.shape[:2]
    wide = 2 * LANES
    for l in range(layers):
        both = jnp.concatenate(
            [own_first(core, mine_ref[l].astype(F32)), own_first(core, theirs_ref[l].astype(F32))], axis=0
        ).astype(BF16)
        for tile in range(own_ref.shape[2] // wide):
            at = slice(tile * wide, (tile + 1) * wide)
            rows = jnp.concatenate([own_ref[l, :, at], in_ref[l, :, at]], axis=0)
            got = jnp.dot(both, rows, preferred_element_type=F32)
            got = (got[:rank] + got[rank:]).astype(BF16)
            out_ref[l, 2 * tile] = got[:, :LANES]
            out_ref[l, 2 * tile + 1] = got[:, LANES:]


def left_of(core, x_own, x_in, mine, theirs):
    layers, _, half = x_in.shape
    rank = mine.shape[1]
    return pl.pallas_call(
        left_body,
        in_specs=[SCALAR, WHOLE, WHOLE, WHOLE, WHOLE],
        out_specs=WHOLE,
        out_shape=pltpu.VMEM((layers, half // LANES, rank, LANES), BF16),
        compiler_params=params(6),
        name="left",
    )(core, near(x_own), near(x_in), near(mine), near(theirs))


def rows_of(p_ref, layer):
    return jnp.concatenate([p_ref[layer, tile] for tile in range(p_ref.shape[1])], axis=1)


def gram_body(p_ref, out_ref):
    rank = p_ref.shape[2]
    for l in range(p_ref.shape[0]):
        rows = rows_of(p_ref, l)
        got = lax.dot_general(rows, rows, TRANSPOSED, preferred_element_type=F32)
        out_ref[:, l * rank : (l + 1) * rank] = got


def gram_of(p_blocks):
    layers, _, rank, _ = p_blocks.shape
    return pl.pallas_call(
        gram_body,
        in_specs=[WHOLE],
        out_specs=WHOLE,
        out_shape=pltpu.VMEM((rank, layers * rank), F32),
        cost_estimate=pl.CostEstimate(flops=2 * rank * p_blocks.size, bytes_accessed=2 * p_blocks.size, transcendentals=0),
        compiler_params=params(8),
        name="gram",
    )(near(p_blocks))


def inner_body(core_ref, own_ref, in_ref, p_ref, out_ref):
    core = core_ref[0]
    tokens = 2 * own_ref.shape[1]
    for l in range(p_ref.shape[0]):
        seen = jnp.concatenate([own_ref[l], in_ref[l]], axis=0)
        got = lax.dot_general(rows_of(p_ref, l), seen, TRANSPOSED, preferred_element_type=F32)
        out_ref[:, l * tokens : (l + 1) * tokens] = own_first(core, got)


def inner_of(core, x_own, x_in, p_blocks):
    layers, tokens, half = x_in.shape
    rank = p_blocks.shape[2]
    return pl.pallas_call(
        inner_body,
        in_specs=[SCALAR, WHOLE, WHOLE, WHOLE],
        out_specs=WHOLE,
        out_shape=pltpu.VMEM((rank, 2 * layers * tokens), F32),
        cost_estimate=pl.CostEstimate(flops=4 * rank * x_in.size, bytes_accessed=6 * x_in.size, transcendentals=0),
        compiler_params=params(8),
        name="inner",
    )(core, near(x_own), near(x_in), near(p_blocks))


def inverse_factors(grams, store):
    rank = grams[0].shape[0]
    height = 8
    blocks = rank // height
    shape = (height, 2 * rank)
    line = lax.broadcasted_iota(jnp.int32, (height, rank), 0)
    column = lax.broadcasted_iota(jnp.int32, (height, rank), 1)
    state = [
        [
            jnp.concatenate(
                [
                    gram[b * height : (b + 1) * height],
                    jnp.where(column == line + b * height, 1.0, 0.0).astype(F32),
                ],
                axis=1,
            )
            for b in range(blocks)
        ]
        for gram in grams
    ]

    def full(value):
        return jnp.broadcast_to(value, shape)

    for at in range(blocks):
        first = at * height
        for index, rows in enumerate(state):
            pivots = [full(rows[at][k : k + 1]) for k in range(height)]
            corners = {
                (k, m): full(pivots[k][:, first + m : first + m + 1]) for k in range(height) for m in range(k, height)
            }
            columns = {
                b: [full(rows[b][:, first + k : first + k + 1]) for k in range(height)]
                for b in range(at + 1, blocks)
            }
            scaled, roots, factors = [], [], {}
            for k in range(height):
                corner, row = corners[k, k], pivots[k]
                for q in range(k):
                    corner = corner - factors[q, k] * factors[q, k]
                roots.append(lax.rsqrt(corner))
                for q in range(k):
                    row = row - factors[q, k] * scaled[q]
                scaled.append(row * roots[k])
                for m in range(k + 1, height):
                    value = corners[k, m]
                    for q in range(k):
                        value = value - factors[q, k] * factors[q, m]
                    factors[k, m] = value * roots[k]
            for k in range(height):
                store(index, first + k, scaled[k][:1, rank:])
            for b in range(at + 1, blocks):
                lower = []
                for k in range(height):
                    value = columns[b][k]
                    for q in range(k):
                        value = value - lower[q] * factors[q, k]
                    lower.append(value * roots[k])
                for k in range(height):
                    rows[b] = rows[b] - lower[k] * scaled[k]


def split3(value):
    high = value.astype(BF16)
    rest = value - high.astype(F32)
    mid = rest.astype(BF16)
    return high, mid, (rest - mid.astype(F32)).astype(BF16)


def factor_body(mine_ref, theirs_ref, inverse_ref):
    layers, rank, _ = inverse_ref.shape
    total = mine_ref[...] + theirs_ref[...]

    def store(layer, row, value):
        inverse_ref[layer, row : row + 1, :] = value

    inverse_factors([total[:, l * rank : (l + 1) * rank] for l in range(layers)], store)


def factor_of(mine, theirs):
    rank, width = mine.shape
    return pl.pallas_call(
        factor_body,
        in_specs=[WHOLE, WHOLE],
        out_specs=WHOLE,
        out_shape=pltpu.VMEM((width // rank, rank, rank), F32),
        cost_estimate=pl.CostEstimate(flops=10**9, bytes_accessed=10**6, transcendentals=0),
        compiler_params=params(8),
        name="factor",
    )(near(mine), near(theirs))


def right_body(scale, inverse_ref, mine_ref, theirs_ref, first_ref, grad_ref, out_ref, held, sems):
    layers, tokens, hidden = grad_ref.shape
    wide = 2 * LANES
    moves = [pltpu.make_async_copy(grad_ref.at[l], held.at[l - 1], sems.at[l - 1]) for l in range(1, layers)]
    for move in moves:
        move.start()
    for l in range(layers):
        at = slice(l * tokens, (l + 1) * tokens)
        left = jnp.dot(
            inverse_ref[l],
            mine_ref[:, at] + theirs_ref[:, at],
            precision=lax.Precision.HIGHEST,
            preferred_element_type=F32,
        ).astype(BF16)
        if l > 0:
            moves[l - 1].wait()
        for tile in range(hidden // wide):
            cut = slice(tile * wide, (tile + 1) * wide)
            rows = first_ref[:, cut] if l == 0 else held[l - 1, :, cut]
            got = jnp.dot(left, rows, preferred_element_type=F32)
            got = (got * scale).astype(BF16)
            out_ref[l, 2 * tile] = got[:, :LANES]
            out_ref[l, 2 * tile + 1] = got[:, LANES:]


def right_of(inverse, mine, theirs, first, grad, scale):
    layers, tokens, hidden = grad.shape
    rank, _ = mine.shape

    def body(*refs):
        right_body(scale, *refs)

    return pl.pallas_call(
        body,
        in_specs=[WHOLE, WHOLE, WHOLE, WHOLE, FAR_MEMORY],
        out_specs=WHOLE,
        out_shape=pltpu.VMEM((layers, hidden // LANES, rank, LANES), BF16),
        scratch_shapes=[pltpu.VMEM((layers - 1, tokens, hidden), BF16), pltpu.SemaphoreType.DMA((layers - 1,))],
        compiler_params=params(10),
        name="right",
    )(near(inverse), near(mine), near(theirs), near(first), stay(grad))


def finish_body(inverse_ref, p_ref, q_ref, hat_ref, new_ref):
    rank = inverse_ref.shape[1]
    wide = 2 * LANES
    for tile in range(q_ref.shape[1]):
        new_ref[0, :, tile * LANES : (tile + 1) * LANES] = q_ref[0, tile].astype(F32)
    stacked = jnp.concatenate(split3(inverse_ref[0]), axis=0)
    for tile in range(p_ref.shape[1] // 2):
        rows = jnp.concatenate([p_ref[0, 2 * tile], p_ref[0, 2 * tile + 1]], axis=1)
        got = jnp.dot(stacked, rows, preferred_element_type=F32)
        got = (got[2 * rank :] + got[rank : 2 * rank]) + got[:rank]
        hat_ref[0, :, tile * wide : (tile + 1) * wide] = got


def finish(inverse, p_blocks, q_blocks):
    layers, p_tiles, rank, _ = p_blocks.shape
    q_tiles = q_blocks.shape[1]
    steps = 2
    return pl.pallas_call(
        finish_body,
        grid=(layers, steps),
        in_specs=[
            pl.BlockSpec((1, rank, rank), lambda l, k: (l, 0, 0)),
            pl.BlockSpec((1, p_tiles // steps, rank, LANES), lambda l, k: (l, k, 0, 0)),
            pl.BlockSpec((1, q_tiles // steps, rank, LANES), lambda l, k: (l, k, 0, 0)),
        ],
        out_specs=[
            pl.BlockSpec((1, rank, p_tiles // steps * LANES), lambda l, k: (l, 0, k)),
            pl.BlockSpec((1, rank, q_tiles // steps * LANES), lambda l, k: (l, 0, k)),
        ],
        out_shape=[
            jax.ShapeDtypeStruct((layers, rank, p_tiles * LANES), F32),
            jax.ShapeDtypeStruct((layers, rank, q_tiles * LANES), F32),
        ],
        compiler_params=params(12),
        name="finish",
    )(inverse, p_blocks, q_blocks)


def exchange(value, axes):
    return lax.all_to_all(value, axes, 0, 0, tiled=True)


def add_up(value):
    return jnp.sum(value.astype(F32), axis=0).astype(BF16)


def copies(value, count):
    return jnp.broadcast_to(value[None], (count, *value.shape))


def sum_over_chips(blocks, group):
    inside, outside = lax.axis_size(group), lax.axis_size(FAR)
    shape = blocks.shape
    chunks = blocks.reshape(inside, -1, LANES)
    chunk = add_up(exchange(chunks, group))
    chunk = add_up(exchange(copies(chunk, outside), FAR))
    return exchange(copies(chunk, inside), group).reshape(shape)


def on_device(x_saved, grad_pre, q_prev):
    token_count = grad_pre.shape[1] * lax.axis_size(CHIPS)
    scale = float(token_count) ** (-0.5)
    core = lax.axis_index(CORE)
    core_array = core.reshape(1)
    x_in = swap(half_of(core_array, x_saved))
    mine, x_own = partial_of(core_array, grad_pre, jnp.swapaxes(q_prev, 1, 2), x_saved)
    theirs = swap(mine)
    p_blocks = sum_over_chips(left_of(core_array, x_own, x_in, mine, theirs), P_NEAR)
    gram = gram_of(p_blocks)
    grad, gram = lax.optimization_barrier((grad_pre, gram))
    inner = inner_of(core_array, x_own, x_in, p_blocks)
    first = fetch(grad)
    inverse = factor_of(gram, swap(gram))
    q_blocks = right_of(inverse, inner, swap(inner), first, grad, scale)
    p_hat, q_new = finish(inverse, p_blocks, sum_over_chips(q_blocks, Q_NEAR))
    return jnp.swapaxes(p_hat, 1, 2), jnp.swapaxes(q_new, 1, 2)


def solution(mesh):
    dims = (4, 2, 4, 4, 2)
    fine = Mesh(mesh.devices.reshape(dims), (*CHIPS, CORE))
    placed = (
        P(None, (*CHIPS, CORE), None),
        P(None, CHIPS, CORE),
        P(None, CORE, None),
    )
    return jax.shard_map(
        on_device,
        mesh=fine,
        in_specs=placed,
        out_specs=(P(None, CORE, None), P(None, CORE, None)),
        check_vma=False,
    )
```

```python
import jax
import jax.numpy as jnp
from jax import lax
from jax.experimental import pallas as pl
from jax.experimental.pallas import tpu as pltpu
from jax.sharding import Mesh
from jax.sharding import PartitionSpec as P

LANES = 128
P_NEAR, Q_NEAR = ("zl", "y", "x"), ("x", "y", "zl")
FAR = ("zh",)
CHIPS = ("zh", "zl", "y", "x")
CORE = "core"
F32, BF16 = jnp.float32, jnp.bfloat16
TRANSPOSED = (((1,), (1,)), ((), ()))
FAR_MEMORY = pl.BlockSpec(memory_space=pltpu.HBM)
WHOLE = pl.BlockSpec(memory_space=pltpu.VMEM)
SCALAR = pl.BlockSpec(memory_space=pltpu.SMEM)


def params(mib):
    return pltpu.CompilerParams(vmem_limit_bytes=mib << 20)


def stay(value):
    return pltpu.with_memory_space_constraint(value, pltpu.HBM)


def near(value):
    return pltpu.with_memory_space_constraint(value, pltpu.VMEM)


def swap(value):
    return lax.ppermute(value, CORE, [(0, 1), (1, 0)])


def half_body(core_ref, x_ref, out_ref, sem):
    half = out_ref.shape[2]
    start = pl.multiple_of((1 - core_ref[0]) * half, LANES)
    move = pltpu.make_async_copy(x_ref.at[:, :, pl.ds(start, half)], out_ref, sem)
    move.start()
    move.wait()


def half_of(core, x):
    layers, tokens, width = x.shape
    return pl.pallas_call(
        half_body,
        in_specs=[SCALAR, FAR_MEMORY],
        out_specs=WHOLE,
        out_shape=pltpu.VMEM((layers, tokens, width // 2), BF16),
        scratch_shapes=[pltpu.SemaphoreType.DMA],
        compiler_params=params(2),
        name="half",
    )(core, stay(x))


def partial_body(core_ref, grad_ref, q_ref, x_ref, out_ref, x_held, grad_held, q_held, sems, x_sem):
    layers, _, hidden = grad_ref.shape
    half = x_held.shape[2]
    steps = sems.shape[2]
    block = hidden // steps
    moves = {}
    for l in range(layers):
        for k in range(steps):
            at = pl.ds(k * block, block)
            for index, (here, held) in enumerate(((q_ref, q_held), (grad_ref, grad_held))):
                moves[l, k, index] = pltpu.make_async_copy(
                    here.at[l, :, at], held.at[l, :, at], sems.at[index, l, k]
                )
                moves[l, k, index].start()
    start = pl.multiple_of(core_ref[0] * half, LANES)
    x_move = pltpu.make_async_copy(x_ref.at[:, :, pl.ds(start, half)], x_held, x_sem)
    x_move.start()
    for l in range(layers):
        total = None
        for k in range(steps):
            moves[l, k, 0].wait()
            moves[l, k, 1].wait()
            at = slice(k * block, (k + 1) * block)
            got = lax.dot_general(
                grad_held[l, :, at], q_held[l, :, at].astype(BF16), TRANSPOSED, preferred_element_type=F32
            )
            total = got if total is None else total + got
        out_ref[l] = total.T.astype(BF16)
    x_move.wait()


def partial_of(core, grad, q_rows, x):
    layers, tokens, hidden = grad.shape
    rank = q_rows.shape[1]
    _, own, width = x.shape
    steps = 4
    return pl.pallas_call(
        partial_body,
        in_specs=[SCALAR, FAR_MEMORY, FAR_MEMORY, FAR_MEMORY],
        out_specs=[WHOLE, WHOLE],
        out_shape=[
            pltpu.VMEM((layers, rank, tokens), BF16),
            pltpu.VMEM((layers, own, width // 2), BF16),
        ],
        scratch_shapes=[
            pltpu.VMEM((layers, tokens, hidden), BF16),
            pltpu.VMEM((layers, rank, hidden), F32),
            pltpu.SemaphoreType.DMA((2, layers, steps)),
            pltpu.SemaphoreType.DMA,
        ],
        compiler_params=params(12),
        name="partial",
    )(core, stay(grad), stay(q_rows), stay(x))


def fetch_body(grad_ref, out_ref, sems):
    moves = [pltpu.make_async_copy(grad_ref.at[l], out_ref.at[l], sems.at[l]) for l in range(out_ref.shape[0])]
    for move in moves:
        move.start()
    for move in moves:
        move.wait()


def fetch(grad):
    return pl.pallas_call(
        fetch_body,
        in_specs=[FAR_MEMORY],
        out_specs=WHOLE,
        out_shape=pltpu.VMEM(grad.shape, BF16),
        scratch_shapes=[pltpu.SemaphoreType.DMA((grad.shape[0],))],
        cost_estimate=pl.CostEstimate(flops=0, bytes_accessed=4 * grad.size, transcendentals=0),
        compiler_params=params(4),
        name="fetch",
    )(stay(grad))


def own_first(core, value):
    mid = value.shape[1] // 2
    low, high = value[:, :mid], value[:, mid:]
    return jnp.concatenate(
        [jnp.where(core == 0, low, high), jnp.where(core == 0, high, low)], axis=1
    )


def left_body(core_ref, own_ref, in_ref, mine_ref, theirs_ref, out_ref):
    core = core_ref[0]
    layers, rank = mine_ref.shape[:2]
    wide = 2 * LANES
    for l in range(layers):
        both = jnp.concatenate(
            [own_first(core, mine_ref[l].astype(F32)), own_first(core, theirs_ref[l].astype(F32))], axis=0
        ).astype(BF16)
        for tile in range(own_ref.shape[2] // wide):
            at = slice(tile * wide, (tile + 1) * wide)
            rows = jnp.concatenate([own_ref[l, :, at], in_ref[l, :, at]], axis=0)
            got = jnp.dot(both, rows, preferred_element_type=F32)
            got = (got[:rank] + got[rank:]).astype(BF16)
            out_ref[l, 2 * tile] = got[:, :LANES]
            out_ref[l, 2 * tile + 1] = got[:, LANES:]


def left_of(core, x_own, x_in, mine, theirs):
    layers, _, half = x_in.shape
    rank = mine.shape[1]
    return pl.pallas_call(
        left_body,
        in_specs=[SCALAR, WHOLE, WHOLE, WHOLE, WHOLE],
        out_specs=WHOLE,
        out_shape=pltpu.VMEM((layers, half // LANES, rank, LANES), BF16),
        compiler_params=params(6),
        name="left",
    )(core, near(x_own), near(x_in), near(mine), near(theirs))


def rows_of(p_ref, layer):
    return jnp.concatenate([p_ref[layer, tile] for tile in range(p_ref.shape[1])], axis=1)


def gram_body(p_ref, out_ref):
    rank = p_ref.shape[2]
    for l in range(p_ref.shape[0]):
        rows = rows_of(p_ref, l)
        got = lax.dot_general(rows, rows, TRANSPOSED, preferred_element_type=F32)
        out_ref[:, l * rank : (l + 1) * rank] = got


def gram_of(p_blocks):
    layers, _, rank, _ = p_blocks.shape
    return pl.pallas_call(
        gram_body,
        in_specs=[WHOLE],
        out_specs=WHOLE,
        out_shape=pltpu.VMEM((rank, layers * rank), F32),
        cost_estimate=pl.CostEstimate(flops=2 * rank * p_blocks.size, bytes_accessed=2 * p_blocks.size, transcendentals=0),
        compiler_params=params(8),
        name="gram",
    )(near(p_blocks))


def inner_body(core_ref, own_ref, in_ref, p_ref, out_ref):
    core = core_ref[0]
    tokens = 2 * own_ref.shape[1]
    for l in range(p_ref.shape[0]):
        seen = jnp.concatenate([own_ref[l], in_ref[l]], axis=0)
        got = lax.dot_general(rows_of(p_ref, l), seen, TRANSPOSED, preferred_element_type=F32)
        out_ref[:, l * tokens : (l + 1) * tokens] = own_first(core, got)


def inner_of(core, x_own, x_in, p_blocks):
    layers, tokens, half = x_in.shape
    rank = p_blocks.shape[2]
    return pl.pallas_call(
        inner_body,
        in_specs=[SCALAR, WHOLE, WHOLE, WHOLE],
        out_specs=WHOLE,
        out_shape=pltpu.VMEM((rank, 2 * layers * tokens), F32),
        cost_estimate=pl.CostEstimate(flops=4 * rank * x_in.size, bytes_accessed=6 * x_in.size, transcendentals=0),
        compiler_params=params(8),
        name="inner",
    )(core, near(x_own), near(x_in), near(p_blocks))


def inverse_factors(grams, store):
    rank = grams[0].shape[0]
    height = 8
    blocks = rank // height
    shape = (height, 2 * rank)
    line = lax.broadcasted_iota(jnp.int32, (height, rank), 0)
    column = lax.broadcasted_iota(jnp.int32, (height, rank), 1)
    state = [
        [
            jnp.concatenate(
                [
                    gram[b * height : (b + 1) * height],
                    jnp.where(column == line + b * height, 1.0, 0.0).astype(F32),
                ],
                axis=1,
            )
            for b in range(blocks)
        ]
        for gram in grams
    ]

    def full(value):
        return jnp.broadcast_to(value, shape)

    for at in range(blocks):
        first = at * height
        for index, rows in enumerate(state):
            pivots = [full(rows[at][k : k + 1]) for k in range(height)]
            corners = {
                (k, m): full(pivots[k][:, first + m : first + m + 1]) for k in range(height) for m in range(k, height)
            }
            columns = {
                b: [full(rows[b][:, first + k : first + k + 1]) for k in range(height)]
                for b in range(at + 1, blocks)
            }
            scaled, roots, factors = [], [], {}
            for k in range(height):
                corner, row = corners[k, k], pivots[k]
                for q in range(k):
                    corner = corner - factors[q, k] * factors[q, k]
                roots.append(lax.rsqrt(corner))
                for q in range(k):
                    row = row - factors[q, k] * scaled[q]
                scaled.append(row * roots[k])
                for m in range(k + 1, height):
                    value = corners[k, m]
                    for q in range(k):
                        value = value - factors[q, k] * factors[q, m]
                    factors[k, m] = value * roots[k]
            for k in range(height):
                store(index, first + k, scaled[k][:1, rank:])
            solved = [None] * height
            for k in reversed(range(height)):
                value = scaled[k]
                for q in range(k + 1, height):
                    value = value - factors[k, q] * solved[q]
                solved[k] = value * roots[k]
            for b in range(at + 1, blocks):
                terms = [columns[b][k] * solved[k] for k in range(height)]
                while len(terms) > 1:
                    terms = [terms[k] + terms[k + 1] for k in range(0, len(terms), 2)]
                rows[b] = rows[b] - terms[0]


def split3(value):
    high = value.astype(BF16)
    rest = value - high.astype(F32)
    mid = rest.astype(BF16)
    return high, mid, (rest - mid.astype(F32)).astype(BF16)


def factor_body(mine_ref, theirs_ref, inverse_ref):
    layers, rank, _ = inverse_ref.shape
    total = mine_ref[...] + theirs_ref[...]

    def store(layer, row, value):
        inverse_ref[layer, row : row + 1, :] = value

    inverse_factors([total[:, l * rank : (l + 1) * rank] for l in range(layers)], store)


def factor_of(mine, theirs):
    rank, width = mine.shape
    return pl.pallas_call(
        factor_body,
        in_specs=[WHOLE, WHOLE],
        out_specs=WHOLE,
        out_shape=pltpu.VMEM((width // rank, rank, rank), F32),
        cost_estimate=pl.CostEstimate(flops=10**9, bytes_accessed=10**6, transcendentals=0),
        compiler_params=params(8),
        name="factor",
    )(near(mine), near(theirs))


def right_body(scale, inverse_ref, mine_ref, theirs_ref, grad_ref, out_ref):
    layers, tokens, hidden = grad_ref.shape
    wide = 2 * LANES
    for l in range(layers):
        at = slice(l * tokens, (l + 1) * tokens)
        left = jnp.dot(
            inverse_ref[l],
            mine_ref[:, at] + theirs_ref[:, at],
            precision=lax.Precision.HIGHEST,
            preferred_element_type=F32,
        ).astype(BF16)
        for tile in range(hidden // wide):
            got = jnp.dot(left, grad_ref[l, :, tile * wide : (tile + 1) * wide], preferred_element_type=F32)
            got = (got * scale).astype(BF16)
            out_ref[l, 2 * tile] = got[:, :LANES]
            out_ref[l, 2 * tile + 1] = got[:, LANES:]


def right_of(inverse, mine, theirs, grad, scale):
    layers, _, hidden = grad.shape
    rank, _ = mine.shape

    def body(*refs):
        right_body(scale, *refs)

    return pl.pallas_call(
        body,
        in_specs=[WHOLE, WHOLE, WHOLE, WHOLE],
        out_specs=WHOLE,
        out_shape=pltpu.VMEM((layers, hidden // LANES, rank, LANES), BF16),
        compiler_params=params(8),
        name="right",
    )(near(inverse), near(mine), near(theirs), near(grad))


def finish_body(inverse_ref, p_ref, q_ref, hat_ref, new_ref):
    rank = inverse_ref.shape[1]
    wide = 2 * LANES
    for tile in range(q_ref.shape[1]):
        new_ref[0, :, tile * LANES : (tile + 1) * LANES] = q_ref[0, tile].astype(F32)
    stacked = jnp.concatenate(split3(inverse_ref[0]), axis=0)
    for tile in range(p_ref.shape[1] // 2):
        rows = jnp.concatenate([p_ref[0, 2 * tile], p_ref[0, 2 * tile + 1]], axis=1)
        got = jnp.dot(stacked, rows, preferred_element_type=F32)
        got = (got[2 * rank :] + got[rank : 2 * rank]) + got[:rank]
        hat_ref[0, :, tile * wide : (tile + 1) * wide] = got


def finish(inverse, p_blocks, q_blocks):
    layers, p_tiles, rank, _ = p_blocks.shape
    q_tiles = q_blocks.shape[1]
    steps = 2
    return pl.pallas_call(
        finish_body,
        grid=(layers, steps),
        in_specs=[
            pl.BlockSpec((1, rank, rank), lambda l, k: (l, 0, 0)),
            pl.BlockSpec((1, p_tiles // steps, rank, LANES), lambda l, k: (l, k, 0, 0)),
            pl.BlockSpec((1, q_tiles // steps, rank, LANES), lambda l, k: (l, k, 0, 0)),
        ],
        out_specs=[
            pl.BlockSpec((1, rank, p_tiles // steps * LANES), lambda l, k: (l, 0, k)),
            pl.BlockSpec((1, rank, q_tiles // steps * LANES), lambda l, k: (l, 0, k)),
        ],
        out_shape=[
            jax.ShapeDtypeStruct((layers, rank, p_tiles * LANES), F32),
            jax.ShapeDtypeStruct((layers, rank, q_tiles * LANES), F32),
        ],
        compiler_params=params(12),
        name="finish",
    )(inverse, p_blocks, q_blocks)


def exchange(value, axes):
    return lax.all_to_all(value, axes, 0, 0, tiled=True)


def add_up(value):
    return jnp.sum(value.astype(F32), axis=0).astype(BF16)


def copies(value, count):
    return jnp.broadcast_to(value[None], (count, *value.shape))


def sum_over_chips(blocks, group):
    inside, outside = lax.axis_size(group), lax.axis_size(FAR)
    shape = blocks.shape
    chunks = blocks.reshape(inside, -1, LANES)
    chunk = add_up(exchange(chunks, group))
    chunk = add_up(exchange(copies(chunk, outside), FAR))
    return exchange(copies(chunk, inside), group).reshape(shape)


def on_device(x_saved, grad_pre, q_prev):
    token_count = grad_pre.shape[1] * lax.axis_size(CHIPS)
    scale = float(token_count) ** (-0.5)
    core = lax.axis_index(CORE)
    core_array = core.reshape(1)
    x_in = swap(half_of(core_array, x_saved))
    mine, x_own = partial_of(core_array, grad_pre, jnp.swapaxes(q_prev, 1, 2), x_saved)
    theirs = swap(mine)
    p_blocks = sum_over_chips(left_of(core_array, x_own, x_in, mine, theirs), P_NEAR)
    gram = gram_of(p_blocks)
    grad, gram = lax.optimization_barrier((grad_pre, gram))
    inner = inner_of(core_array, x_own, x_in, p_blocks)
    held = fetch(grad)
    inverse = factor_of(gram, swap(gram))
    q_blocks = right_of(inverse, inner, swap(inner), held, scale)
    p_hat, q_new = finish(inverse, p_blocks, sum_over_chips(q_blocks, Q_NEAR))
    return jnp.swapaxes(p_hat, 1, 2), jnp.swapaxes(q_new, 1, 2)


def solution(mesh):
    dims = (4, 2, 4, 4, 2)
    fine = Mesh(mesh.devices.reshape(dims), (*CHIPS, CORE))
    placed = (
        P(None, (*CHIPS, CORE), None),
        P(None, CHIPS, CORE),
        P(None, CORE, None),
    )
    return jax.shard_map(
        on_device,
        mesh=fine,
        in_specs=placed,
        out_specs=(P(None, CORE, None), P(None, CORE, None)),
        check_vma=False,
    )
```
